32 devices in a mesh: tm: 8 (over z, core), box: 4 (over y, x).
Axes of the slice: x: 2, y: 2, z: 4, core: 2. Of those that a mesh axis runs over, the one named last changes fastest.
Arguments:
- traces: bfloat16 [6, 128, 65536], P(None, 'tm', 'box'), may hold values from -6 to 6
- projection: bfloat16 [4, 128, 128, 128], P('box', 'tm'), may hold values from -0.5 to 0.5
- owner_route: int32 [4, 128, 1], P('box', 'tm'), may hold values from 0 to 3; in each aligned block of 16 rows (0 to 15, 16 to 31, ..., all dimensions but the last counted through in order) at most 5 rows name the same one
- face_slot: int32 [4, 128, 1], P('box', 'tm'), may hold values from 0 to 3
- face_weight: float32 [128, 128], P(('tm', 'box')), may hold values from 0.2 to 2
Outputs:
- face_load: bfloat16 [128, 6, 128, 128], P(('tm', 'box'))
The draws below stay inside these ranges and needn't reach their ends.
Inputs may be any that keep to these rules, and one draw needn't show every extreme that they name: `owner_route`: in the aligned blocks of 16 rows (the rows of one device), no owner is named by more than 5 rows, a bound that some block reaches.
All inputs are finite; a program needn't handle non-finite values.
Results may differ from the reference program's by a relative error of at most 0.005.
Values may be sent and summed in bfloat16 or wider, within the bound.
No kernel may reach another device: no remote copies, remote signals or barrier semaphores. Data moves between devices by JAX's collectives and lax.ppermute only.
A program may use at most 192 MiB of HBM per device.

```python
import math
import jax
import jax.numpy as jnp
import numpy as np
from jax import lax

COMP = 6
NODES = 128
SAMPLES = 128
BDEV = 16
FCAP = 4
CAP = 5
POINTS = 65536
FACES = 128
N_TM = 8
N_BOX = 4


def set_ends(result, own_key, low, high):
    spot = [jax.random.randint(jax.random.fold_in(own_key, axis), (), 0, length) for axis, length in enumerate(result.shape)]
    longest = result.shape.index(max(result.shape))
    beside = spot[:longest] + [(spot[longest] + 1) % result.shape[longest]] + spot[longest + 1:]
    return result.at[tuple(spot)].set(low).at[tuple(beside)].set(high)


def shard_levels(key, dims, cuts, smallest, top_value):
    level = 1.0
    for position, blocks in cuts:
        heights = jax.random.uniform(jax.random.fold_in(jax.random.fold_in(key, 6), position), (blocks,), jnp.float32, smallest / len(cuts), top_value / len(cuts))
        level = level * jnp.repeat(jnp.exp(heights), dims[position] // blocks).reshape((-1,) + (1,) * (len(dims) - 1 - position))
    return level


def routed_block(rng, own, number, rows, number_of, top, bound, skew):
    ranking = jax.random.permutation(rng, number_of)
    heavy_load, ordinary = shares(number_of, rows * top, bound, skew, True), shares(number_of, rows * top, bound, skew, False)
    places = jnp.arange(number_of)

    def named(tallies, turn):
        used = int((tallies > 0).sum())
        fixed = max(1, used // 4)
        passed = fixed + (places - fixed + turn * (used - fixed)) % max(1, number_of - fixed)
        return jnp.zeros((number_of,), jnp.int32).at[ranking[jnp.where(places < fixed, places, passed)]].set(jnp.asarray(tallies, jnp.int32))

    tallies = jnp.where(number % 4 == 0, named(heavy_load, number // 4), named(ordinary, number - number // 4 - 1))
    mixed = jax.random.permutation(jax.random.fold_in(own, 3), number_of)
    giver, receiver = mixed[0:number_of // 2 * 2:2], mixed[1:number_of // 2 * 2:2]
    room = jnp.minimum(tallies[giver] - 1, bound - tallies[receiver]) // 2
    room = jnp.where((giver == ranking[0]) | (receiver == ranking[0]) | (tallies[receiver] == 0), 0, jnp.maximum(room, 0))
    passed = jax.random.randint(jax.random.fold_in(own, 4), (number_of // 2,), 0, 1 << 20) % (room + 1)
    tallies = tallies.at[giver].add(-passed).at[receiver].add(passed)
    labels = jnp.searchsorted(jnp.cumsum(tallies), jnp.arange(rows * top), side="right").astype(jnp.int32)
    grid = labels.reshape(top, rows).T
    grid = grid[jax.random.permutation(jax.random.fold_in(own, 1), rows)]
    turn = jax.random.randint(jax.random.fold_in(own, 2), (rows, 1), 0, top)
    return jnp.take_along_axis(grid, (jnp.arange(top)[None, :] + turn) % top, axis=1)


def shares(count, total, limit, lean, full):
    loads = [(1 << 20) // math.isqrt(standing ** lean) + 1 for standing in range(1, count + 1)]
    largest = limit if full else min(limit, max(-(-total // count), total * loads[0] // sum(loads)))
    least = 1 if total - largest >= count - 1 else 0
    holding, spare = [largest] + [least] * (count - 1), total - largest - least * (count - 1)
    while spare > 0:
        candidates = [i for i in range(1, count) if holding[i] < largest] or [i for i in range(1, count) if holding[i] < limit]
        whole, budget = sum([loads[i] for i in candidates]), spare
        for i in candidates:
            addition = min(limit - holding[i], max(1, budget * loads[i] // whole), spare)
            holding[i] = holding[i] + addition
            spare = spare - addition
    return np.array(holding)


def scatter_about(key, dims, deviation, reach, split=(), kind=jnp.bfloat16):
    values = jax.random.normal(key, dims, jnp.float32) * deviation
    if len(split) > 0:
        values = shard_levels(key, dims, split, -0.22, 0.18) * values
    return jnp.clip(values, min=-reach, max=reach).astype(kind)


def setup_inputs(seed: int = 0) -> dict:
    key_of = jax.random.split(jax.random.key(seed), 6)
    traces = scatter_about(key_of[0], (COMP, SAMPLES, POINTS), 1.0, 6.0, ((1, 8), (2, 4)))
    projection = scatter_about(key_of[1], (N_BOX, N_TM * BDEV, NODES, NODES), NODES ** -0.5, 0.5, ((0, 4), (1, 8)))
    owner_route_keys = jax.random.split(jax.random.fold_in(key_of[2], 1), N_BOX * (N_TM * BDEV) // BDEV)
    owner_route_turns = jax.random.permutation(jax.random.fold_in(key_of[2], 3), N_BOX * (N_TM * BDEV) // BDEV)
    owner_route = jax.vmap(lambda own, number: routed_block(jax.random.fold_in(key_of[2], 2), own, number, BDEV, N_BOX, 1, CAP, 2))(owner_route_keys, owner_route_turns).reshape((N_BOX, N_TM * BDEV, 1))
    face_slot = set_ends(jax.random.randint(key_of[3], (N_BOX, N_TM * BDEV, 1), 0, FCAP), jax.random.fold_in(key_of[3], 1), 0, FCAP - 1).astype(jnp.int32)
    face_weight = jnp.clip(jnp.exp(math.log(2.0) - 2.3025851 * jax.random.uniform(key_of[4], (FACES, NODES), jnp.float32) ** shard_levels(key_of[4], (FACES, NODES), ((0, 32),), -0.2, 0.2)), 0.2, 2.0)
    return dict(traces=traces, projection=projection, owner_route=owner_route, face_slot=face_slot, face_weight=face_weight)


def reference(traces, projection, owner_route, face_slot, face_weight):
    series = traces.reshape(COMP, SAMPLES, N_BOX, N_TM, BDEV, NODES)
    matrices = projection.reshape(N_BOX, N_TM, BDEV, NODES, NODES)
    owners = owner_route.reshape(N_BOX, N_TM, BDEV)
    slots = face_slot.reshape(N_BOX, N_TM, BDEV)
    weights = face_weight.reshape(N_TM, N_BOX * FCAP, NODES)

    def one_row(row):
        part = lax.dynamic_index_in_dim(series, row, 3, keepdims=False)
        mats = lax.dynamic_index_in_dim(matrices, row, 1, keepdims=False)
        faces = jnp.einsum("csbjn,bjnm->bjcsm", part.astype(jnp.float32), mats.astype(jnp.float32))
        faces = faces.astype(jnp.bfloat16).astype(jnp.float32)
        row_owner = lax.dynamic_index_in_dim(owners, row, 1, keepdims=False)
        row_slot = lax.dynamic_index_in_dim(slots, row, 1, keepdims=False)
        target = (row_owner * FCAP + row_slot).reshape(-1).astype(jnp.int32)
        summed = jax.ops.segment_sum(faces.reshape(N_BOX * BDEV, COMP, SAMPLES, NODES), target, num_segments=N_BOX * FCAP)
        scale = lax.dynamic_index_in_dim(weights, row, 0, keepdims=False)
        return (summed * scale[:, None, None, :]).astype(jnp.bfloat16)

    rows = lax.map(one_row, jnp.arange(N_TM, dtype=jnp.int32))
    return rows.reshape(FACES, COMP, SAMPLES, NODES)
```

```python
import functools

import jax
import jax.numpy as jnp
import numpy as np
from jax import lax
from jax.experimental import pallas as pl
from jax.experimental.pallas import tpu as pltpu
from jax.sharding import PartitionSpec as P

CORES = 2
IDS = 4


def pick_kernel(ids, x_ref, o_ref):
    o_ref[...] = x_ref[...]


def pick(ids, traces, chips, width):
    comp, samples, _ = traces.shape
    block = (comp, samples, width)
    return pl.pallas_call(
        pick_kernel,
        grid_spec=pltpu.PrefetchScalarGridSpec(
            num_scalar_prefetch=1,
            grid=(chips,),
            in_specs=[pl.BlockSpec(block, lambda i, ids: (0, 0, CORES * i + 1 - ids[0]))],
            out_specs=pl.BlockSpec(block, lambda i, ids: (0, 0, i)),
        ),
        out_shape=jax.ShapeDtypeStruct((comp, samples, width * chips), traces.dtype),
        name="pick",
    )(ids, traces)


def interpolate_kernel(turn, count, boxes, ids, targets, own_ref, far_ref, *rest):
    sources, outs, (mats, acc, sem) = rest[:count], rest[count:count + boxes], rest[count + boxes:]
    core, box, which = ids[turn * IDS], ids[turn * IDS + 2], ids[turn * IDS + 3]
    for i, source in enumerate(sources):
        @pl.when(which == i)
        def _():
            pltpu.make_async_copy(source, mats, sem).start()
    acc[...] = jnp.zeros_like(acc)
    pltpu.make_async_copy(sources[0], mats, sem).wait()
    blocks, nodes, _ = mats.shape
    comp, samples, _ = own_ref.shape
    slots = acc.shape[0] // boxes
    for j in range(blocks):
        target = targets[j]
        for ref, half in ((own_ref, core), (far_ref, 1 - core)):
            x = ref[:, :, j * nodes:(j + 1) * nodes]
            if samples % 16:
                x = x.astype(jnp.float32).reshape(comp * samples, nodes).astype(x.dtype)
            else:
                x = x.reshape(comp * samples, nodes)
            y = jnp.dot(x, mats[j], preferred_element_type=jnp.float32)
            acc[target, :, half] += y.reshape(comp, samples, nodes)
    for d, out in enumerate(outs):
        for s in range(slots):
            part = acc[(box ^ d) * slots + s]
            out[s] = part.reshape(comp, 2 * samples, nodes).astype(out.dtype)


def interpolate(turn, ids, targets, traces, far, sources, boxes, slots):
    blocks, nodes, _ = sources[0].shape
    comp, samples, _ = traces.shape
    width = blocks * nodes
    block = (comp, samples, width)
    shape = (slots, comp, 2 * samples, nodes)
    n = blocks * comp * CORES * samples
    return pl.pallas_call(
        functools.partial(interpolate_kernel, turn, len(sources), boxes),
        grid_spec=pltpu.PrefetchScalarGridSpec(
            num_scalar_prefetch=2,
            grid=(1,),
            in_specs=[
                pl.BlockSpec(block, lambda i, ids, t: (0, 0, CORES * ids[turn * IDS + 1] + ids[turn * IDS])),
                pl.BlockSpec(block, lambda i, ids, t: (0, 0, ids[turn * IDS + 1])),
            ] + [pl.BlockSpec(memory_space=pl.ANY)] * len(sources),
            out_specs=[pl.BlockSpec(shape, lambda i, ids, t: (0, 0, 0, 0))] * boxes,
            scratch_shapes=[
                pltpu.VMEM(sources[0].shape, sources[0].dtype),
                pltpu.VMEM((boxes * slots, comp, CORES, samples, nodes), jnp.float32),
                pltpu.SemaphoreType.DMA,
            ],
        ),
        out_shape=[
            jax.ShapeDtypeStruct(shape, jnp.bfloat16 if d else jnp.float32) for d in range(boxes)
        ],
        compiler_params=pltpu.CompilerParams(vmem_limit_bytes=32 * 2**20),
        cost_estimate=pl.CostEstimate(flops=2 * n * nodes * nodes, bytes_accessed=4 * n * nodes + 2 * blocks * nodes * nodes, transcendentals=0),
        name="interpolate",
    )(ids, targets, traces, far, *sources)


def total_kernel(*refs):
    out = refs[-1]
    for s in range(out.shape[0]):
        total = refs[0][s]
        for ref in refs[1:-1]:
            total = total + ref[s].astype(jnp.float32)
        out[s] = total.astype(out.dtype)


def total(parts, dtype):
    return pl.pallas_call(
        total_kernel,
        out_shape=jax.ShapeDtypeStruct(parts[0].shape, dtype),
        compiler_params=pltpu.CompilerParams(vmem_limit_bytes=32 * 2**20),
        cost_estimate=pl.CostEstimate(flops=parts[0].size * len(parts), bytes_accessed=2 * parts[0].size * (len(parts) + 2), transcendentals=0),
        name="total",
    )(*parts)


def finish_kernel(chips, ids, weight_ref, *refs):
    out = refs[-1]
    slots, _, length, _ = refs[0].shape
    for turn in range(chips):
        at = pl.ds(pl.multiple_of(ids[turn * IDS + 1] * length, length), length)
        for s in range(slots):
            value = refs[turn][s].astype(jnp.float32) * weight_ref[s:s + 1, :][None]
            out[s, :, at, :] = value.astype(out.dtype)


def finish(ids, weight, pieces):
    slots, comp, length, nodes = pieces[0].shape
    chips = len(pieces)
    shape = (slots, comp, length * chips, nodes)
    whole = lambda s: pl.BlockSpec(s, lambda i, ids: (0,) * len(s))
    return pl.pallas_call(
        functools.partial(finish_kernel, chips),
        grid_spec=pltpu.PrefetchScalarGridSpec(
            num_scalar_prefetch=1,
            grid=(1,),
            in_specs=[whole(weight.shape)] + [whole(p.shape) for p in pieces],
            out_specs=whole(shape),
        ),
        out_shape=jax.ShapeDtypeStruct(shape, jnp.bfloat16),
        compiler_params=pltpu.CompilerParams(vmem_limit_bytes=32 * 2**20),
        name="finish",
    )(ids, weight, *pieces)


def plan(chips, boxes):
    ways = [[(0, 0)]]
    for r in range(1, chips):
        ways.append(sorted({((z ^ r) > z, abs((z ^ r) - z)) for z in range(chips)}))
    table = np.zeros((chips, CORES, boxes, chips, IDS), np.int32)
    for z in range(chips):
        for r in range(chips):
            way = ((z ^ r) > z, abs((z ^ r) - z))
            for c in range(CORES):
                for b in range(boxes):
                    table[z, c, b, r] = (c, z ^ r, b, ways[r].index(way))
    return ways, table.reshape(chips * CORES, boxes, chips * IDS)


def per_device(chips, boxes, traces, projection, owner_route, face_slot, face_weight):
    ways, table = plan(chips, boxes)
    matrices = projection[0]
    blocks, nodes, _ = matrices.shape
    slots = face_weight.shape[0]
    ids = jnp.asarray(table)[lax.axis_index("tm"), lax.axis_index("box")]

    def along(x, pairs):
        return lax.ppermute(x, "tm", [(a * CORES + c, b * CORES + c) for a, b in pairs for c in range(CORES)])

    arrived = {(0, 0): matrices}
    up, down = matrices, matrices
    for k in range(1, chips):
        up = along(up, [(z, z + 1) for z in range(k - 1, chips - 1)])
        down = along(down, [(z + 1, z) for z in range(chips - k)])
        arrived[(False, k)], arrived[(True, k)] = up, down

    targets = owner_route[0, :, 0] * slots + face_slot[0, :, 0]
    far = lax.ppermute(
        pick(ids, traces, chips, blocks * nodes), "tm", [(i, i ^ 1) for i in range(chips * CORES)]
    )
    pieces = []
    for r in range(chips):
        turn = [(z, z ^ r) for z in range(chips)]
        named = along(targets, turn) if r else targets
        parts = interpolate(r, ids, named, traces, far, [arrived[w] for w in ways[r]], boxes, slots)
        parts = [parts[0]] + [
            lax.ppermute(parts[d], "box", [(b, b ^ d) for b in range(boxes)]) for d in range(1, boxes)
        ]
        summed = total(parts, jnp.bfloat16 if r else jnp.float32)
        pieces.append(along(summed, turn) if r else summed)
    return finish(ids, face_weight, pieces)


def solution(mesh):
    chips, boxes = mesh.shape["tm"] // CORES, mesh.shape["box"]
    return jax.shard_map(
        functools.partial(per_device, chips, boxes),
        mesh=mesh,
        in_specs=(
            P(None, "tm", "box"),
            P("box", "tm", None, None),
            P("box", "tm", None),
            P("box", "tm", None),
            P(("tm", "box"), None),
        ),
        out_specs=P(("tm", "box"), None, None, None),
        check_vma=False,
    )
```

```python
import functools

import jax
import jax.numpy as jnp
from jax import lax
from jax.experimental import pallas as pl
from jax.experimental.pallas import tpu as pltpu
from jax.sharding import PartitionSpec as P

CORES = 2
TAIL = 16
LIMIT = pltpu.CompilerParams(vmem_limit_bytes=32 * 2**20)


def place():
    me = lax.axis_index("tm")
    return me // CORES, lax.rem(me, CORES), lax.axis_index("box")


def pack_kernel(slots, mats_ref, owner_ref, slot_ref, out_ref):
    rows, nodes = mats_ref.shape
    blocks = owner_ref.shape[1]
    out_ref[:rows, :] = mats_ref[...]
    target = (owner_ref[...] * slots + slot_ref[...]).astype(jnp.float32)
    row = jnp.concatenate([target, jnp.zeros((1, nodes - blocks), jnp.float32)], axis=1)
    out_ref[rows:, :] = jnp.broadcast_to(row, (TAIL, nodes)).astype(out_ref.dtype)


def pack(matrices, owners, slot_of, slots):
    rows, nodes = matrices.shape
    return pl.pallas_call(
        functools.partial(pack_kernel, slots),
        out_shape=jax.ShapeDtypeStruct((rows + TAIL, nodes), matrices.dtype),
        name="pack",
    )(matrices, owners, slot_of)


def interpolate_kernel(turn, boxes, blocks, own_hbm, far_hbm, mats_hbm, *rest):
    outs, (own, far, mats, acc, sems) = rest[:boxes], rest[boxes:]
    chip, core, box = place()
    comp, samples, width = own.shape
    nodes = mats.shape[1]
    slots = acc.shape[0] // boxes
    at = pl.ds(pl.multiple_of(((chip ^ turn) * CORES + core) * width, width), width)
    copies = [
        pltpu.make_async_copy(mats_hbm, mats, sems.at[0]),
        pltpu.make_async_copy(own_hbm.at[:, :, at], own, sems.at[1]),
        pltpu.make_async_copy(far_hbm.at[:, :, at], far, sems.at[2]),
    ]
    for copy in copies:
        copy.start()
    acc[...] = jnp.zeros_like(acc)
    for copy in copies:
        copy.wait()
    named = mats[blocks * nodes:, :].astype(jnp.float32)
    for j in range(blocks):
        target = named[0, j].astype(jnp.int32)
        for ref, half in ((own, core), (far, 1 - core)):
            x = ref[:, :, j * nodes:(j + 1) * nodes]
            if samples % 16:
                x = x.astype(jnp.float32).reshape(comp * samples, nodes).astype(x.dtype)
            else:
                x = x.reshape(comp * samples, nodes)
            y = jnp.dot(x, mats[j * nodes:(j + 1) * nodes, :], preferred_element_type=jnp.float32)
            acc[target, :, half] += y.reshape(comp, samples, nodes)
    for d, out in enumerate(outs):
        for s in range(slots):
            part = acc[(box ^ d) * slots + s]
            out[s] = part.reshape(comp, CORES * samples, nodes).astype(out.dtype)


def interpolate(turn, traces, far, mats, blocks, boxes, slots):
    nodes = mats.shape[1]
    comp, samples, _ = traces.shape
    width = blocks * nodes
    shape = (slots, comp, CORES * samples, nodes)
    return pl.pallas_call(
        functools.partial(interpolate_kernel, turn, boxes, blocks),
        in_specs=[pl.BlockSpec(memory_space=pl.ANY)] * 3,
        out_specs=[pl.BlockSpec(memory_space=pltpu.VMEM)] * boxes,
        scratch_shapes=[
            pltpu.VMEM((comp, samples, width), traces.dtype),
            pltpu.VMEM((comp, samples, width), traces.dtype),
            pltpu.VMEM(mats.shape, mats.dtype),
            pltpu.VMEM((boxes * slots, comp, CORES, samples, nodes), jnp.float32),
            pltpu.SemaphoreType.DMA((3,)),
        ],
        out_shape=[
            jax.ShapeDtypeStruct(shape, jnp.bfloat16 if d else jnp.float32) for d in range(boxes)
        ],
        compiler_params=LIMIT,
        name="interpolate",
    )(traces, far, mats)


def total_kernel(*refs):
    out = refs[-1]
    for s in range(out.shape[0]):
        value = refs[0][s]
        for ref in refs[1:-1]:
            value = value + ref[s].astype(jnp.float32)
        out[s] = value.astype(out.dtype)


def total(parts, dtype):
    return pl.pallas_call(
        total_kernel,
        out_shape=jax.ShapeDtypeStruct(parts[0].shape, dtype),
        compiler_params=LIMIT,
        name="total",
    )(*parts)


def finish_kernel(weight_ref, *refs):
    out = refs[-1]
    chip, _, _ = place()
    slots, _, length, _ = refs[0].shape
    for turn, ref in enumerate(refs[:-1]):
        at = pl.ds(pl.multiple_of((chip ^ turn) * length, length), length)
        for s in range(slots):
            value = ref[s].astype(jnp.float32) * weight_ref[s:s + 1, :][None]
            out[s, :, at, :] = value.astype(out.dtype)


def finish(weight, pieces):
    slots, comp, length, nodes = pieces[0].shape
    return pl.pallas_call(
        finish_kernel,
        out_shape=jax.ShapeDtypeStruct((slots, comp, length * len(pieces), nodes), jnp.bfloat16),
        compiler_params=LIMIT,
        name="finish",
    )(weight, *pieces)


def per_device(chips, boxes, traces, projection, owner_route, face_slot, face_weight):
    _, blocks, nodes, _ = projection.shape
    slots = face_weight.shape[0]

    def turned(x, r):
        pairs = [(z * CORES + c, (z ^ r) * CORES + c) for z in range(chips) for c in range(CORES)]
        return lax.ppermute(x, "tm", pairs)

    mats = pack(
        projection.reshape(blocks * nodes, nodes),
        owner_route.reshape(1, blocks), face_slot.reshape(1, blocks), slots,
    )
    far = lax.ppermute(traces, "tm", [(i, i ^ 1) for i in range(chips * CORES)])
    barrier = lax.optimization_barrier

    def crossed(r, mats):
        parts = interpolate(r, traces, far, mats, blocks, boxes, slots)
        return [parts[0]] + [
            lax.ppermute(parts[d], "box", [(b, b ^ d) for b in range(boxes)]) for d in range(1, boxes)
        ]

    pieces = {0: total(crossed(0, mats), jnp.float32)}
    first, arrived = turned(mats, 1), None
    for r in range(2, chips, 2):
        even = turned(mats, r)
        even, first, pieces[r - 2] = barrier((even, first, pieces[r - 2]))
        odd = turned(even, 1)
        parts = crossed(r, even)
        if r == 2:
            late = crossed(1, first)
        summed = total(parts, jnp.bfloat16)
        odd, summed = barrier((odd, summed))
        pieces[r] = turned(summed, r)
        parts = crossed(r + 1, odd)
        if r == 2:
            late[0], parts[0] = barrier((late[0], parts[0]))
            pieces[1] = turned(total(late, jnp.bfloat16), 1)
        pieces[r], parts[0] = barrier((pieces[r], parts[0]))
        pieces[r + 1] = turned(total(parts, jnp.bfloat16), r + 1)
    return finish(face_weight, [pieces[r] for r in range(chips)])


def solution(mesh):
    chips, boxes = mesh.shape["tm"] // CORES, mesh.shape["box"]
    return jax.shard_map(
        functools.partial(per_device, chips, boxes),
        mesh=mesh,
        in_specs=(
            P(None, "tm", "box"),
            P("box", "tm", None, None),
            P("box", "tm", None),
            P("box", "tm", None),
            P(("tm", "box"), None),
        ),
        out_specs=P(("tm", "box"), None, None, None),
        check_vma=False,
    )
```

```python
import functools

import jax
import jax.numpy as jnp
from jax import lax
from jax.experimental import pallas as pl
from jax.experimental.pallas import tpu as pltpu
from jax.sharding import PartitionSpec as P

CORES = 2
LIMIT = pltpu.CompilerParams(vmem_limit_bytes=32 * 2**20)

ORDER = {('name', 1, 0): [('face', 0, 0)], ('name', 2, 0): [('face', 0, 0)], ('name', 3, 0): [('face', 0, 0)], ('mats', 3, 0): [('mats', 1, 0), ('name', 1, 0), ('name', 2, 0), ('sum', 0, 0)], ('face', 3, 0): [('sum', 2, 0)], ('home', 2, 0): [('mats', 3, 0)], ('sum', 1, 0): [('face', 3, 0)], ('sum', 3, 0): [('home', 2, 0)]}


def place():
    me = lax.axis_index("tm")
    return me // CORES, lax.rem(me, CORES), lax.axis_index("box")


def interpolate_kernel(turn, boxes, blocks, named, own_hbm, far_hbm, mats_hbm, *rest):
    outs, (own, far, mats, acc, sems) = rest[:boxes], rest[boxes:]
    chip, core, box = place()
    comp, samples, width = own.shape
    nodes = mats.shape[1]
    slots = acc.shape[0] // boxes
    at = pl.ds(pl.multiple_of(((chip ^ turn) * CORES + core) * width, width), width)
    copies = [
        pltpu.make_async_copy(mats_hbm, mats, sems.at[0]),
        pltpu.make_async_copy(own_hbm.at[:, :, at], own, sems.at[1]),
        pltpu.make_async_copy(far_hbm.at[:, :, at], far, sems.at[2]),
    ]
    for copy in copies:
        copy.start()
    acc[...] = jnp.zeros_like(acc)
    for copy in copies:
        copy.wait()
    named_row = named[...]
    for j in range(blocks):
        target = named_row[0, j]
        for ref, half in ((own, core), (far, 1 - core)):
            x = ref[:, :, j * nodes:(j + 1) * nodes]
            if samples % 16:
                x = x.astype(jnp.float32).reshape(comp * samples, nodes).astype(x.dtype)
            else:
                x = x.reshape(comp * samples, nodes)
            y = jnp.dot(x, mats[j * nodes:(j + 1) * nodes, :], preferred_element_type=jnp.float32)
            acc[target, :, half] += y.reshape(comp, samples, nodes)
    for d, out in enumerate(outs):
        for s in range(slots):
            part = acc[(box ^ d) * slots + s]
            out[s] = part.reshape(comp, CORES * samples, nodes).astype(out.dtype)


def interpolate(turn, named, traces, far, mats, blocks, boxes, slots):
    nodes = mats.shape[1]
    comp, samples, _ = traces.shape
    width = blocks * nodes
    shape = (slots, comp, CORES * samples, nodes)
    return pl.pallas_call(
        functools.partial(interpolate_kernel, turn, boxes, blocks),
        in_specs=[pl.BlockSpec(memory_space=pltpu.VMEM)] + [pl.BlockSpec(memory_space=pl.ANY)] * 3,
        out_specs=[pl.BlockSpec(memory_space=pltpu.VMEM)] * boxes,
        scratch_shapes=[
            pltpu.VMEM((comp, samples, width), traces.dtype),
            pltpu.VMEM((comp, samples, width), traces.dtype),
            pltpu.VMEM(mats.shape, mats.dtype),
            pltpu.VMEM((boxes * slots, comp, CORES, samples, nodes), jnp.float32),
            pltpu.SemaphoreType.DMA((3,)),
        ],
        out_shape=[
            jax.ShapeDtypeStruct(shape, jnp.bfloat16 if d else jnp.float32) for d in range(boxes)
        ],
        compiler_params=LIMIT,
        name="interpolate",
    )(named, traces, far, mats)


def total_kernel(*refs):
    out = refs[-1]
    for s in range(out.shape[0]):
        value = refs[0][s]
        for ref in refs[1:-1]:
            value = value + ref[s].astype(jnp.float32)
        out[s] = value.astype(out.dtype)


def total(parts, dtype):
    return pl.pallas_call(
        total_kernel,
        out_shape=jax.ShapeDtypeStruct(parts[0].shape, dtype),
        compiler_params=LIMIT,
        name="total",
    )(*parts)


def finish_kernel(turns, count, weight_ref, *refs):
    pieces, out, (scratch, sems) = refs[:count], refs[-3], refs[-2:]
    chip, _, _ = place()
    _, _, length, _ = pieces[0].shape
    copies, first = [], 0
    for i, (turn, piece) in enumerate(zip(turns, pieces)):
        number = piece.shape[0]
        first = 0 if i and turn != turns[i - 1] else first
        for s in range(number):
            value = piece[s].astype(jnp.float32) * weight_ref[first + s:first + s + 1, :][None]
            scratch[i, s] = value.astype(scratch.dtype)
        at = pl.ds(pl.multiple_of((chip ^ turn) * length, length), length)
        copies.append(pltpu.make_async_copy(
            scratch.at[i, :number], out.at[first:first + number, :, at, :], sems.at[i]
        ))
        copies[-1].start()
        first += number
    for copy in copies:
        copy.wait()


def finish(weight, turns, pieces, chips, earlier=None):
    slots, _ = weight.shape
    number, comp, length, nodes = pieces[0].shape
    whole = pl.BlockSpec(memory_space=pltpu.VMEM)
    rest = [] if earlier is None else [earlier]
    return pl.pallas_call(
        functools.partial(finish_kernel, turns, len(pieces)),
        in_specs=[whole] * (1 + len(pieces)) + [pl.BlockSpec(memory_space=pl.ANY)] * len(rest),
        out_specs=pl.BlockSpec(memory_space=pl.ANY),
        scratch_shapes=[
            pltpu.VMEM((len(pieces), number, comp, length, nodes), jnp.bfloat16),
            pltpu.SemaphoreType.DMA((len(pieces),)),
        ],
        out_shape=jax.ShapeDtypeStruct((slots, comp, length * chips, nodes), jnp.bfloat16),
        input_output_aliases={1 + len(pieces): 0} if rest else {},
        compiler_params=LIMIT,
        name="finish",
    )(weight, *pieces, *rest)


def per_device(chips, boxes, traces, projection, owner_route, face_slot, face_weight):
    _, blocks, nodes, _ = projection.shape
    slots = face_weight.shape[0]
    whole = projection.reshape(blocks * nodes, nodes)
    targets = owner_route.reshape(1, blocks) * slots + face_slot.reshape(1, blocks)
    made = {}

    def along(x, turn):
        pairs = [(z * CORES + c, (z ^ turn) * CORES + c) for z in range(chips) for c in range(CORES)]
        return lax.ppermute(x, "tm", pairs)

    def make(kind, turn=0, d=0):
        def wait(x):
            others = [get(*other) for other in ORDER.get((kind, turn, d), ())]
            others = [y[0] if isinstance(y, (list, tuple)) else y for y in others]
            return lax.optimization_barrier((x, *others))[0] if others else x

        if kind == "mats":
            if turn < 2:
                return along(wait(whole), turn) if turn else whole
            return along(wait(get("mats", turn - 1)), 1) if turn % 2 else along(wait(whole), turn)
        if kind == "name":
            return along(wait(targets), turn) if turn else targets
        if kind == "far":
            return lax.ppermute(wait(traces), "tm", [(j, j ^ 1) for j in range(chips * CORES)])
        if kind == "face":
            mats = wait(get("mats", turn))
            return interpolate(turn, get("name", turn), traces, get("far"), mats, blocks, boxes, slots)
        if kind == "cross":
            return lax.ppermute(wait(get("face", turn)[d]), "box", [(b, b ^ d) for b in range(boxes)])
        if kind == "sum":
            mine = wait(get("face", turn)[0])
            return total([mine] + [get("cross", turn, d) for d in range(1, boxes)], jnp.bfloat16 if turn else jnp.float32)
        if kind == "home":
            return along(wait(get("sum", turn)), turn) if turn else get("sum", 0)

    def get(kind, turn=0, d=0):
        key = (kind, turn, d)
        if key not in made:
            made[key] = make(*key)
        return made[key]

    last = chips - 1
    out = finish(face_weight, range(last), [get("home", r) for r in range(last)], chips)
    return finish(face_weight, [last], [get("home", last)], chips, out)


def solution(mesh):
    chips, boxes = mesh.shape["tm"] // CORES, mesh.shape["box"]
    return jax.shard_map(
        functools.partial(per_device, chips, boxes),
        mesh=mesh,
        in_specs=(
            P(None, "tm", "box"),
            P("box", "tm", None, None),
            P("box", "tm", None),
            P("box", "tm", None),
            P(("tm", "box"), None),
        ),
        out_specs=P(("tm", "box"), None, None, None),
        check_vma=False,
    )
```

```python
import functools

import jax
import jax.numpy as jnp
from jax import lax
from jax.experimental import pallas as pl
from jax.experimental.pallas import tpu as pltpu
from jax.sharding import PartitionSpec as P

CORES = 2
LIMIT = pltpu.CompilerParams(vmem_limit_bytes=32 * 2**20)

ORDER = {('name', 1, 0): [('face', 0, 0)], ('name', 2, 0): [('face', 0, 0)], ('name', 3, 0): [('face', 0, 0)], ('mats', 3, 0): [('mats', 1, 0), ('name', 1, 0), ('name', 2, 0), ('sum', 0, 0)], ('home', 2, 0): [('mats', 3, 0)], ('sum', 3, 0): [('home', 2, 0)]}


def place():
    me = lax.axis_index("tm")
    return me // CORES, lax.rem(me, CORES), lax.axis_index("box")


def interpolate_kernel(turn, boxes, blocks, named, own_hbm, far_hbm, mats_hbm, *rest):
    outs, (own, far, mats, acc, sems) = rest[:boxes], rest[boxes:]
    chip, core, box = place()
    comp, samples, width = own.shape
    nodes = mats.shape[1]
    slots = acc.shape[0] // boxes
    at = pl.ds(pl.multiple_of(((chip ^ turn) * CORES + core) * width, width), width)
    copies = [
        pltpu.make_async_copy(mats_hbm, mats, sems.at[0]),
        pltpu.make_async_copy(own_hbm.at[:, :, at], own, sems.at[1]),
        pltpu.make_async_copy(far_hbm.at[:, :, at], far, sems.at[2]),
    ]
    for copy in copies:
        copy.start()
    acc[...] = jnp.zeros_like(acc)
    for copy in copies:
        copy.wait()
    named_row = named[...]
    for j in range(blocks):
        target = named_row[0, j]
        for ref, half in ((own, core), (far, 1 - core)):
            x = ref[:, :, j * nodes:(j + 1) * nodes]
            if samples % 16:
                x = x.astype(jnp.float32).reshape(comp * samples, nodes).astype(x.dtype)
            else:
                x = x.reshape(comp * samples, nodes)
            y = jnp.dot(x, mats[j * nodes:(j + 1) * nodes, :], preferred_element_type=jnp.float32)
            acc[target, :, half] += y.reshape(comp, samples, nodes)
    for d, out in enumerate(outs):
        for s in range(slots):
            part = acc[(box ^ d) * slots + s]
            out[s] = part.reshape(comp, CORES * samples, nodes).astype(out.dtype)


def interpolate(turn, named, traces, far, mats, blocks, boxes, slots):
    nodes = mats.shape[1]
    comp, samples, _ = traces.shape
    width = blocks * nodes
    shape = (slots, comp, CORES * samples, nodes)
    return pl.pallas_call(
        functools.partial(interpolate_kernel, turn, boxes, blocks),
        in_specs=[pl.BlockSpec(memory_space=pltpu.VMEM)] + [pl.BlockSpec(memory_space=pl.ANY)] * 3,
        out_specs=[pl.BlockSpec(memory_space=pltpu.VMEM)] * boxes,
        scratch_shapes=[
            pltpu.VMEM((comp, samples, width), traces.dtype),
            pltpu.VMEM((comp, samples, width), traces.dtype),
            pltpu.VMEM(mats.shape, mats.dtype),
            pltpu.VMEM((boxes * slots, comp, CORES, samples, nodes), jnp.float32),
            pltpu.SemaphoreType.DMA((3,)),
        ],
        out_shape=[
            jax.ShapeDtypeStruct(shape, jnp.bfloat16 if d else jnp.float32) for d in range(boxes)
        ],
        compiler_params=LIMIT,
        name="interpolate",
    )(named, traces, far, mats)


def total_kernel(*refs):
    out = refs[-1]
    for s in range(out.shape[0]):
        value = refs[0][s]
        for ref in refs[1:-1]:
            value = value + ref[s].astype(jnp.float32)
        out[s] = value.astype(out.dtype)


def total(parts, dtype):
    return pl.pallas_call(
        total_kernel,
        out_shape=jax.ShapeDtypeStruct(parts[0].shape, dtype),
        compiler_params=LIMIT,
        name="total",
    )(*parts)


def finish_kernel(turns, count, weight_ref, *refs):
    pieces, out, (scratch, sems) = refs[:count], refs[-3], refs[-2:]
    chip, _, _ = place()
    _, _, length, _ = pieces[0].shape
    copies, first = [], 0
    for i, (turn, piece) in enumerate(zip(turns, pieces)):
        number = piece.shape[0]
        first = 0 if i and turn != turns[i - 1] else first
        for s in range(number):
            value = piece[s].astype(jnp.float32) * weight_ref[first + s:first + s + 1, :][None]
            scratch[i, s] = value.astype(scratch.dtype)
        at = pl.ds(pl.multiple_of((chip ^ turn) * length, length), length)
        copies.append(pltpu.make_async_copy(
            scratch.at[i, :number], out.at[first:first + number, :, at, :], sems.at[i]
        ))
        copies[-1].start()
        first += number
    for copy in copies:
        copy.wait()


def finish(weight, turns, pieces, chips, earlier=None):
    slots, _ = weight.shape
    number, comp, length, nodes = pieces[0].shape
    whole = pl.BlockSpec(memory_space=pltpu.VMEM)
    rest = [] if earlier is None else [earlier]
    return pl.pallas_call(
        functools.partial(finish_kernel, turns, len(pieces)),
        in_specs=[whole] * (1 + len(pieces)) + [pl.BlockSpec(memory_space=pl.ANY)] * len(rest),
        out_specs=pl.BlockSpec(memory_space=pl.ANY),
        scratch_shapes=[
            pltpu.VMEM((len(pieces), number, comp, length, nodes), jnp.bfloat16),
            pltpu.SemaphoreType.DMA((len(pieces),)),
        ],
        out_shape=jax.ShapeDtypeStruct((slots, comp, length * chips, nodes), jnp.bfloat16),
        input_output_aliases={1 + len(pieces): 0} if rest else {},
        compiler_params=LIMIT,
        name="finish",
    )(weight, *pieces, *rest)


def per_device(chips, boxes, traces, projection, owner_route, face_slot, face_weight):
    _, blocks, nodes, _ = projection.shape
    slots = face_weight.shape[0]
    whole = projection.reshape(blocks * nodes, nodes)
    targets = owner_route.reshape(1, blocks) * slots + face_slot.reshape(1, blocks)
    made = {}

    def along(x, turn):
        pairs = [(z * CORES + c, (z ^ turn) * CORES + c) for z in range(chips) for c in range(CORES)]
        return lax.ppermute(x, "tm", pairs)

    def make(kind, turn=0, d=0):
        def wait(x):
            others = [get(*other) for other in ORDER.get((kind, turn, d), ())]
            others = [y[0] if isinstance(y, (list, tuple)) else y for y in others]
            return lax.optimization_barrier((x, *others))[0] if others else x

        if kind == "mats":
            if turn < 2:
                return along(wait(whole), turn) if turn else whole
            return along(wait(get("mats", turn - 1)), 1) if turn % 2 else along(wait(whole), turn)
        if kind == "name":
            return along(wait(targets), turn) if turn else targets
        if kind == "far":
            return lax.ppermute(wait(traces), "tm", [(j, j ^ 1) for j in range(chips * CORES)])
        if kind == "face":
            mats = wait(get("mats", turn))
            return interpolate(turn, get("name", turn), traces, get("far"), mats, blocks, boxes, slots)
        if kind == "cross":
            return lax.ppermute(wait(get("face", turn)[d]), "box", [(b, b ^ d) for b in range(boxes)])
        if kind == "sum":
            mine = wait(get("face", turn)[0])
            return total([mine] + [get("cross", turn, d) for d in range(1, boxes)], jnp.bfloat16 if turn else jnp.float32)
        if kind == "home":
            return along(wait(get("sum", turn)), turn) if turn else get("sum", 0)

    def get(kind, turn=0, d=0):
        key = (kind, turn, d)
        if key not in made:
            made[key] = make(*key)
        return made[key]

    last = chips - 1
    out = finish(face_weight, range(last), [get("home", r) for r in range(last)], chips)
    return finish(face_weight, [last], [get("home", last)], chips, out)


def solution(mesh):
    chips, boxes = mesh.shape["tm"] // CORES, mesh.shape["box"]
    return jax.shard_map(
        functools.partial(per_device, chips, boxes),
        mesh=mesh,
        in_specs=(
            P(None, "tm", "box"),
            P("box", "tm", None, None),
            P("box", "tm", None),
            P("box", "tm", None),
            P(("tm", "box"), None),
        ),
        out_specs=P(("tm", "box"), None, None, None),
        check_vma=False,
    )
```

```python
import functools

import jax
import jax.numpy as jnp
from jax import lax
from jax.experimental import pallas as pl
from jax.experimental.pallas import tpu as pltpu
from jax.sharding import PartitionSpec as P

CORES = 2
LIMIT = pltpu.CompilerParams(vmem_limit_bytes=32 * 2**20)

ORDER = {('name', 1, 0): [('face', 0, 0)], ('name', 2, 0): [('face', 0, 0)], ('name', 3, 0): [('face', 0, 0)], ('mats', 3, 0): [('mats', 1, 0), ('name', 1, 0), ('name', 2, 0), ('sum', 0, 0)], ('home', 2, 0): [('mats', 3, 0)], ('sum', 3, 0): [('home', 2, 0)]}


def place():
    me = lax.axis_index("tm")
    return me // CORES, lax.rem(me, CORES), lax.axis_index("box")


def interpolate_kernel(turn, boxes, blocks, named, traces, far, mats, *rest):
    outs, acc = rest[:boxes], rest[boxes]
    chip, core, box = place()
    comp, samples, _ = traces.shape
    nodes = mats.shape[1]
    slots = acc.shape[0] // boxes
    start = ((chip ^ turn) * CORES + core) * blocks * nodes
    acc[...] = jnp.zeros_like(acc)
    named_row = named[...]
    for j in range(blocks):
        target = named_row[0, j]
        at = pl.ds(pl.multiple_of(start + j * nodes, nodes), nodes)
        for ref, half in ((traces, core), (far, 1 - core)):
            x = ref[:, :, at]
            if samples % 16:
                x = x.astype(jnp.float32).reshape(comp * samples, nodes).astype(x.dtype)
            else:
                x = x.reshape(comp * samples, nodes)
            y = jnp.dot(x, mats[j * nodes:(j + 1) * nodes, :], preferred_element_type=jnp.float32)
            acc[target, :, half] += y.reshape(comp, samples, nodes)
    for d, out in enumerate(outs):
        for s in range(slots):
            part = acc[(box ^ d) * slots + s]
            out[s] = part.reshape(comp, CORES * samples, nodes).astype(out.dtype)


def interpolate(turn, named, traces, far, mats, blocks, boxes, slots):
    nodes = mats.shape[1]
    comp, samples, _ = traces.shape
    shape = (slots, comp, CORES * samples, nodes)
    return pl.pallas_call(
        functools.partial(interpolate_kernel, turn, boxes, blocks),
        in_specs=[pl.BlockSpec(memory_space=pltpu.VMEM)] * 4,
        out_specs=[pl.BlockSpec(memory_space=pltpu.VMEM)] * boxes,
        scratch_shapes=[pltpu.VMEM((boxes * slots, comp, CORES, samples, nodes), jnp.float32)],
        out_shape=[
            jax.ShapeDtypeStruct(shape, jnp.bfloat16 if d else jnp.float32) for d in range(boxes)
        ],
        compiler_params=LIMIT,
        name="interpolate",
    )(named, traces, far, mats)


def total_kernel(*refs):
    out = refs[-1]
    for s in range(out.shape[0]):
        value = refs[0][s]
        for ref in refs[1:-1]:
            value = value + ref[s].astype(jnp.float32)
        out[s] = value.astype(out.dtype)


def total(parts, dtype):
    return pl.pallas_call(
        total_kernel,
        out_shape=jax.ShapeDtypeStruct(parts[0].shape, dtype),
        compiler_params=LIMIT,
        name="total",
    )(*parts)


def finish_kernel(turns, count, weight_ref, *refs):
    pieces, out, (scratch, sems) = refs[:count], refs[-3], refs[-2:]
    chip, _, _ = place()
    _, _, length, _ = pieces[0].shape
    copies, first = [], 0
    for i, (turn, piece) in enumerate(zip(turns, pieces)):
        number = piece.shape[0]
        first = 0 if i and turn != turns[i - 1] else first
        for s in range(number):
            value = piece[s].astype(jnp.float32) * weight_ref[first + s:first + s + 1, :][None]
            scratch[i, s] = value.astype(scratch.dtype)
        at = pl.ds(pl.multiple_of((chip ^ turn) * length, length), length)
        copies.append(pltpu.make_async_copy(
            scratch.at[i, :number], out.at[first:first + number, :, at, :], sems.at[i]
        ))
        copies[-1].start()
        first += number
    for copy in copies:
        copy.wait()


def finish(weight, turns, pieces, chips, earlier=None):
    slots, _ = weight.shape
    number, comp, length, nodes = pieces[0].shape
    whole = pl.BlockSpec(memory_space=pltpu.VMEM)
    rest = [] if earlier is None else [earlier]
    return pl.pallas_call(
        functools.partial(finish_kernel, turns, len(pieces)),
        in_specs=[whole] * (1 + len(pieces)) + [pl.BlockSpec(memory_space=pl.ANY)] * len(rest),
        out_specs=pl.BlockSpec(memory_space=pl.ANY),
        scratch_shapes=[
            pltpu.VMEM((len(pieces), number, comp, length, nodes), jnp.bfloat16),
            pltpu.SemaphoreType.DMA((len(pieces),)),
        ],
        out_shape=jax.ShapeDtypeStruct((slots, comp, length * chips, nodes), jnp.bfloat16),
        input_output_aliases={1 + len(pieces): 0} if rest else {},
        compiler_params=LIMIT,
        name="finish",
    )(weight, *pieces, *rest)


def per_device(chips, boxes, traces, projection, owner_route, face_slot, face_weight):
    _, blocks, nodes, _ = projection.shape
    slots = face_weight.shape[0]
    whole = projection.reshape(blocks * nodes, nodes)
    targets = owner_route.reshape(1, blocks) * slots + face_slot.reshape(1, blocks)
    made = {}

    def along(x, turn):
        pairs = [(z * CORES + c, (z ^ turn) * CORES + c) for z in range(chips) for c in range(CORES)]
        return lax.ppermute(x, "tm", pairs)

    def make(kind, turn=0, d=0):
        def wait(x):
            others = [get(*other) for other in ORDER.get((kind, turn, d), ())]
            others = [y[0] if isinstance(y, (list, tuple)) else y for y in others]
            return lax.optimization_barrier((x, *others))[0] if others else x

        if kind == "mats":
            if turn < 2:
                return along(wait(whole), turn) if turn else whole
            return along(wait(get("mats", turn - 1)), 1) if turn % 2 else along(wait(whole), turn)
        if kind == "name":
            return along(wait(targets), turn) if turn else targets
        if kind == "far":
            return lax.ppermute(wait(traces), "tm", [(j, j ^ 1) for j in range(chips * CORES)])
        if kind == "face":
            mats = wait(get("mats", turn))
            return interpolate(turn, get("name", turn), traces, get("far"), mats, blocks, boxes, slots)
        if kind == "cross":
            return lax.ppermute(wait(get("face", turn)[d]), "box", [(b, b ^ d) for b in range(boxes)])
        if kind == "sum":
            mine = wait(get("face", turn)[0])
            return total([mine] + [get("cross", turn, d) for d in range(1, boxes)], jnp.bfloat16 if turn else jnp.float32)
        if kind == "home":
            return along(wait(get("sum", turn)), turn) if turn else get("sum", 0)

    def get(kind, turn=0, d=0):
        key = (kind, turn, d)
        if key not in made:
            made[key] = make(*key)
        return made[key]

    last = chips - 1
    out = finish(face_weight, range(last), [get("home", r) for r in range(last)], chips)
    return finish(face_weight, [last], [get("home", last)], chips, out)


def solution(mesh):
    chips, boxes = mesh.shape["tm"] // CORES, mesh.shape["box"]
    return jax.shard_map(
        functools.partial(per_device, chips, boxes),
        mesh=mesh,
        in_specs=(
            P(None, "tm", "box"),
            P("box", "tm", None, None),
            P("box", "tm", None),
            P("box", "tm", None),
            P(("tm", "box"), None),
        ),
        out_specs=P(("tm", "box"), None, None, None),
        check_vma=False,
    )
```
